32 devices in a mesh: groups: 2 (over x), seq: 4 (over y, core), tp: 4 (over z).
Axes of the slice: x: 2, y: 2, z: 4, core: 2. Of those that a mesh axis runs over, the one named last changes fastest.
Arguments:
- hidden: bfloat16 [768, 16384], P(('groups', 'tp'), 'seq'), parts along dimension 0, may hold values from -7 to 7
- w_query: bfloat16 [16384, 16384], P('seq', 'tp'), may hold values from -0.1875 to 0.1875
- w_key: bfloat16 [16384, 1024], P('seq', 'tp'), may hold values from -0.046875 to 0.046875
- w_value: bfloat16 [16384, 1024], P('seq', 'tp'), may hold values from -0.046875 to 0.046875
- w_out: bfloat16 [16384, 16384], P('tp', 'seq'), may hold values from -0.046875 to 0.046875
- vert_blocks: int32 [256, 3], P(('groups', 'tp')), parts along dimension 0, may hold values from 0 to 2, as said below
- vert_count: int32 [256], P(('groups', 'tp')), parts along dimension 0, may hold values from 1 to 3, as said below
- slash_offsets: int32 [256, 3], P(('groups', 'tp')), parts along dimension 0, may hold values from 0 to 2, as said below
- slash_count: int32 [256], P(('groups', 'tp')), parts along dimension 0, may hold values from 1 to 3, as said below
Outputs:
- attn_out: bfloat16 [768, 16384], P(('groups', 'tp'), 'seq'), parts along dimension 0
The draws below stay inside these ranges and needn't reach their ends.
There are 2 independent parts, one for each index of `groups`. The reference program is written for one: setup_inputs(seed, part) draws one part's arguments, and reference() takes and returns one part's arrays. A program takes and returns all parts, laid end to end along the dimension named above; an argument that names none is the same for every part. Nothing has to cross between parts.
Inputs may be any that keep to these rules, and one draw needn't show every extreme that they name: `vert_blocks`: each head's 3 entries are distinct block indices; only the first vert_count of them are used. `vert_count`: some head has exactly 3. `slash_offsets`: each head's 3 entries are distinct and the first is 0; only the first slash_count of them are used. `slash_count`: some head has exactly 3.
All inputs are finite; a program needn't handle non-finite values.
Results may differ from the reference program's by a relative error of at most 0.012.
The reference program's roundings to bfloat16 on the way count: a program that leaves them out, or rounds other values in their place, can miss the bound.
Values may be sent and summed in bfloat16 or wider, within the bound.
A program may use at most 192 MiB of HBM per device.

```python
import math
import jax
import jax.numpy as jnp
from jax import lax

D = 16384
HEADS = 128
KV_HEADS = 8
HEAD_DIM = 128
BLOCK = 128
VERT = 3
SLASH = 3
TOKENS = 384


def draw_hidden(key, part):
    key = jax.random.fold_in(key, 1)
    first_key = jax.random.fold_in(key, 0)
    values = jax.random.normal(first_key, (TOKENS, D), jnp.float32)
    return jnp.clip(values, -6.0, 6.0).astype(jnp.bfloat16)


def live_counts(key, most):
    first_key, second_key = jax.random.split(key)
    counts = jax.random.randint(first_key, (HEADS,), 1, most + 1)
    chosen = jax.random.randint(second_key, (), 0, HEADS)
    return jnp.where(jnp.arange(HEADS) == chosen, most, counts).astype(jnp.int32)


def draw_vert_blocks(key, part):
    key = jax.random.fold_in(key, 2)
    head_keys = jax.random.split(key, HEADS)
    picked = jax.vmap(lambda head_key: jax.random.permutation(head_key, TOKENS // BLOCK)[:VERT])(head_keys)
    return picked.astype(jnp.int32)


def draw_vert_count(key, part):
    key = jax.random.fold_in(key, 3)
    return live_counts(key, VERT)


def draw_slash_offsets(key, part):
    key = jax.random.fold_in(key, 4)
    head_keys = jax.random.split(key, HEADS)

    def one_list(head_key):
        rest = 1 + jax.random.permutation(head_key, TOKENS // BLOCK - 1)[:SLASH - 1]
        return jnp.concatenate([jnp.zeros((1,), jnp.int32), rest.astype(jnp.int32)])
    return jax.vmap(one_list)(head_keys).astype(jnp.int32)


def draw_slash_count(key, part):
    key = jax.random.fold_in(key, 5)
    return live_counts(key, SLASH)


def level_of(stream_key, dims, pieces, smallest, top_value):
    level, own = 1.0, jax.random.fold_in(stream_key, 6)
    for position, blocks in pieces:
        steps = jnp.exp(jax.random.uniform(jax.random.fold_in(own, position), (blocks,), jnp.float32, smallest / len(pieces), top_value / len(pieces)))
        level = level * jnp.repeat(steps, dims[position] // blocks).reshape([-1 if axis == position else 1 for axis in range(len(dims))])
    return level


def noise(key, dims, width, bound, pieces=(), kind=jnp.bfloat16):
    array = jax.random.normal(key, dims, jnp.float32) * width
    if len(pieces) > 0:
        array = level_of(key, dims, pieces, -0.22, 0.18) * array
    return jnp.clip(array, min=-bound, max=bound).astype(kind)


def setup_inputs(seed: int = 0, part: int = 0) -> dict:
    keys = jax.random.split(jax.random.key(seed), 10)
    own_keys = jax.random.split(jax.random.fold_in(keys[9], part), 10)
    return {
        "hidden": draw_hidden(jax.random.fold_in(jax.random.fold_in(keys[9], part), 71), part),
        "w_query": noise(keys[1], (D, HEADS * HEAD_DIM), (D // 16) ** -0.5, 0.1875, ((0, 4), (1, 4))),
        "w_key": noise(keys[2], (D, KV_HEADS * HEAD_DIM), D ** -0.5, 0.046875, ((0, 4), (1, 4))),
        "w_value": noise(keys[3], (D, KV_HEADS * HEAD_DIM), D ** -0.5, 0.046875, ((0, 4), (1, 4))),
        "w_out": noise(keys[4], (HEADS * HEAD_DIM, D), (HEADS * HEAD_DIM) ** -0.5, 0.046875, ((0, 4), (1, 4))),
        "vert_blocks": draw_vert_blocks(jax.random.fold_in(jax.random.fold_in(keys[9], part), 71), part),
        "vert_count": draw_vert_count(jax.random.fold_in(jax.random.fold_in(keys[9], part), 71), part),
        "slash_offsets": draw_slash_offsets(jax.random.fold_in(jax.random.fold_in(keys[9], part), 71), part),
        "slash_count": draw_slash_count(jax.random.fold_in(jax.random.fold_in(keys[9], part), 71), part),
    }


NEG_FILL = -1e+30

def rope_tables(positions):
    pair_index = jnp.arange(HEAD_DIM // 2, dtype=jnp.float32)
    base_freq = jnp.exp(-(2.0 * pair_index / HEAD_DIM) * jnp.log(500000.0))
    wavelength = 2.0 * jnp.pi / base_freq
    smooth = (8192.0 / wavelength - 1.0) / 3.0
    blended = (1.0 - smooth) * base_freq / 8.0 + smooth * base_freq
    scaled = jnp.where(wavelength < 2048.0, base_freq, jnp.where(wavelength > 8192.0, base_freq / 8.0, blended))
    angles = positions.astype(jnp.float32)[:, None] * scaled[None, :]
    return (jnp.cos(angles), jnp.sin(angles))

def rotate_pairs(values, cos_table, sin_table):
    paired = values.reshape(values.shape[:-1] + (HEAD_DIM // 2, 2))
    real_part = paired[..., 0]
    imag_part = paired[..., 1]
    turned = jnp.stack([real_part * cos_table - imag_part * sin_table, real_part * sin_table + imag_part * cos_table], axis=-1)
    return turned.reshape(values.shape)

def visible_blocks(vert_list, vert_live, slash_list, slash_live, blocks):
    block_ids = jnp.arange(blocks, dtype=jnp.int32)
    vert_in_use = jnp.arange(VERT, dtype=jnp.int32) < vert_live
    slash_in_use = jnp.arange(SLASH, dtype=jnp.int32) < slash_live
    vert_member = jnp.any((vert_list[:, None] == block_ids[None, :]) & vert_in_use[:, None], axis=0)
    slash_member = jnp.any((slash_list[:, None] == block_ids[None, :]) & slash_in_use[:, None], axis=0)
    distance = block_ids[:, None] - block_ids[None, :]
    behind = slash_member[jnp.clip(distance, 0, blocks - 1)]
    return (distance >= 0) & (vert_member[None, :] | behind)

def reference(hidden, w_query, w_key, w_value, w_out, vert_blocks, vert_count, slash_offsets, slash_count):
    tokens = hidden.shape[0]
    blocks = tokens // BLOCK
    group_size = HEADS // KV_HEADS
    cos_table, sin_table = rope_tables(jnp.arange(tokens, dtype=jnp.int32))
    query_raw = jnp.dot(hidden, w_query, preferred_element_type=jnp.float32).reshape(tokens, HEADS, HEAD_DIM)
    key_raw = jnp.dot(hidden, w_key, preferred_element_type=jnp.float32).reshape(tokens, KV_HEADS, HEAD_DIM)
    value_raw = jnp.dot(hidden, w_value, preferred_element_type=jnp.float32)
    queries = rotate_pairs(query_raw, cos_table[:, None, :], sin_table[:, None, :]).astype(jnp.bfloat16).transpose(1, 0, 2)
    keys_all = rotate_pairs(key_raw, cos_table[:, None, :], sin_table[:, None, :]).astype(jnp.bfloat16).transpose(1, 0, 2)
    values_all = value_raw.astype(jnp.bfloat16).reshape(tokens, KV_HEADS, HEAD_DIM).transpose(1, 0, 2)
    token_ids = jnp.arange(tokens, dtype=jnp.int32)
    causal = token_ids[None, :] <= token_ids[:, None]
    score_scale = 1.0 / math.sqrt(HEAD_DIM)

    def one_head(head_id):
        shared = head_id // group_size
        block_mask = visible_blocks(vert_blocks[head_id], vert_count[head_id], slash_offsets[head_id], slash_count[head_id], blocks)
        visible = jnp.repeat(jnp.repeat(block_mask, BLOCK, axis=0), BLOCK, axis=1) & causal
        scores = jnp.dot(queries[head_id], keys_all[shared].T, preferred_element_type=jnp.float32) * score_scale
        masked = jnp.where(visible, scores, NEG_FILL)
        row_max = lax.optimization_barrier(jnp.max(masked, axis=1, keepdims=True))
        weights = jnp.where(visible, jnp.exp(masked - row_max), 0.0)
        weights_low = (weights / lax.optimization_barrier(jnp.sum(weights, axis=1, keepdims=True))).astype(jnp.bfloat16)
        return jnp.dot(weights_low, values_all[shared], preferred_element_type=jnp.float32).astype(jnp.bfloat16)
    attended = lax.map(one_head, jnp.arange(HEADS, dtype=jnp.int32))
    merged = attended.transpose(1, 0, 2).reshape(tokens, HEADS * HEAD_DIM)
    return jnp.dot(merged, w_out, preferred_element_type=jnp.float32).astype(jnp.bfloat16)
```

```python
import functools
import math

import jax
import jax.numpy as jnp
from jax import lax
from jax.experimental import pallas as pl
from jax.experimental.pallas import tpu as pltpu
from jax.sharding import PartitionSpec as P

HEAD_DIM = 128
BLOCK = 128
VERT = 3
SLASH = 3


NEG_FILL = -1e30


def rope_tables(positions):
    pair_index = jnp.arange(HEAD_DIM // 2, dtype=jnp.float32)
    base_freq = jnp.exp(-(2.0 * pair_index / HEAD_DIM) * jnp.log(500000.0))
    wavelength = 2.0 * jnp.pi / base_freq
    smooth = (8192.0 / wavelength - 1.0) / 3.0
    blended = (1.0 - smooth) * base_freq / 8.0 + smooth * base_freq
    scaled = jnp.where(
        wavelength < 2048.0, base_freq, jnp.where(wavelength > 8192.0, base_freq / 8.0, blended)
    )
    angles = positions.astype(jnp.float32)[:, None] * scaled[None, :]
    return (jnp.cos(angles), jnp.sin(angles))


def attend_kernel(
    heads_here,
    query_ref,
    pair_ref,
    cos_ref,
    sin_ref,
    vert_ref,
    vert_live_ref,
    slash_ref,
    slash_live_ref,
    out_ref,
    key_ref,
    value_ref,
):
    tokens = query_ref.shape[0]
    blocks = tokens // BLOCK
    score_scale = 1.0 / math.sqrt(HEAD_DIM)
    even = lax.broadcasted_iota(jnp.int32, (tokens, HEAD_DIM), 1) % 2 == 0

    def rotate(raw):
        swapped = jnp.where(
            even, pltpu.roll(raw, HEAD_DIM - 1, 1), pltpu.roll(raw, 1, 1)
        )
        return (raw * cos_ref[...] + swapped * sin_ref[...]).astype(jnp.bfloat16)

    @pl.when(pl.program_id(0) == 0)
    def _():
        key_ref[...] = rotate(pair_ref[:, :HEAD_DIM])
        value_ref[...] = pair_ref[:, HEAD_DIM:].astype(jnp.bfloat16)

    head = lax.axis_index("seq") * heads_here + pl.program_id(0)
    vert_live = vert_live_ref[head]
    slash_live = slash_live_ref[head]

    def listed(list_ref, live, slots, block):
        found = jnp.int32(0)
        for slot in range(slots):
            hit = (list_ref[head, slot] == block) & (live > slot)
            found = found | hit.astype(jnp.int32)
        return found

    vert_member = [listed(vert_ref, vert_live, VERT, block) for block in range(blocks)]
    slash_member = [listed(slash_ref, slash_live, SLASH, block) for block in range(blocks)]
    query = rotate(query_ref[...])
    causal = lax.broadcasted_iota(jnp.int32, (BLOCK, BLOCK), 1) <= lax.broadcasted_iota(
        jnp.int32, (BLOCK, BLOCK), 0
    )
    for row in range(blocks):
        width = (row + 1) * BLOCK
        scores = (
            lax.dot_general(
                query[row * BLOCK : width],
                key_ref[:width],
                (((1,), (1,)), ((), ())),
                preferred_element_type=jnp.float32,
            )
            * score_scale
        )
        masked = []
        for block in range(row + 1):
            visible = vert_member[block] | slash_member[row - block]
            bias = jnp.where(visible > 0, jnp.float32(0.0), jnp.float32(NEG_FILL))
            piece = scores[:, block * BLOCK : (block + 1) * BLOCK] + bias
            if block == row:
                piece = jnp.where(causal, piece, NEG_FILL)
            masked.append(piece)
        masked = masked[0] if row == 0 else jnp.concatenate(masked, axis=1)
        row_max = jnp.max(masked, axis=1, keepdims=True)
        weights = jnp.exp(masked - row_max)
        row_sum = jnp.sum(weights, axis=1, keepdims=True)
        weights_low = (weights / row_sum).astype(jnp.bfloat16)
        out_ref[row * BLOCK : width, :] = jnp.dot(
            weights_low, value_ref[:width], preferred_element_type=jnp.float32
        ).astype(jnp.bfloat16)


def attend(query_all, pair_all, cos_full, sin_full, lists):
    tokens, width = query_all.shape
    heads_here = width // HEAD_DIM
    whole = lambda head: (0, 0)
    one_head = lambda head: (0, head)
    return pl.pallas_call(
        functools.partial(attend_kernel, heads_here),
        grid=(heads_here,),
        out_shape=jax.ShapeDtypeStruct((tokens, width), jnp.bfloat16),
        in_specs=[
            pl.BlockSpec((tokens, HEAD_DIM), one_head),
            pl.BlockSpec((tokens, 2 * HEAD_DIM), whole),
            pl.BlockSpec((tokens, HEAD_DIM), whole),
            pl.BlockSpec((tokens, HEAD_DIM), whole),
        ]
        + [pl.BlockSpec(memory_space=pltpu.SMEM)] * 4,
        out_specs=pl.BlockSpec((tokens, HEAD_DIM), one_head),
        scratch_shapes=[
            pltpu.VMEM((tokens, HEAD_DIM), jnp.bfloat16),
            pltpu.VMEM((tokens, HEAD_DIM), jnp.bfloat16),
        ],
        compiler_params=pltpu.CompilerParams(vmem_limit_bytes=40 * 1024 * 1024),
    )(query_all, pair_all, cos_full, sin_full, *lists)


def swap_with(value, bit, size):
    return lax.ppermute(value, "seq", [(rank, rank ^ bit) for rank in range(size)])


def scatter_heads(segments, size, rank):
    bit = 1
    while bit < size:
        low = (rank // bit) % 2 == 0
        count = len(segments) // 2
        width = segments[0].shape[1]
        kept = [jnp.where(low, segments[2 * i], segments[2 * i + 1]) for i in range(count)]
        sent = [jnp.where(low, segments[2 * i + 1], segments[2 * i]) for i in range(count)]
        got = swap_with(jnp.concatenate(sent, axis=1), bit, size)
        segments = [kept[i] + got[:, i * width : (i + 1) * width] for i in range(count)]
        bit *= 2
    return segments[0]


def gather_heads(piece, size, rank):
    segments = [piece]
    width = piece.shape[1]
    bit = size // 2
    while bit >= 1:
        low = (rank // bit) % 2 == 0
        got = swap_with(jnp.concatenate(segments, axis=1), bit, size)
        wider = []
        for i, mine in enumerate(segments):
            other = got[:, i * width : (i + 1) * width]
            wider += [jnp.where(low, mine, other), jnp.where(low, other, mine)]
        segments = wider
        bit //= 2
    return jnp.concatenate(segments, axis=1)


def on_device(
    hidden, w_query, w_key, w_value, w_out, vert_blocks, vert_count, slash_offsets, slash_count
):
    seq_size = lax.axis_size("seq")
    seq_rank = lax.axis_index("seq")
    ring = lax.axis_size("tp")
    place = lax.axis_index("tp")
    rows = hidden.shape[0]
    tokens = rows * ring
    head_width = w_query.shape[1] // seq_size
    pairs = w_key.shape[1] // HEAD_DIM
    share = seq_size // pairs
    down = [(i, (i - 1) % ring) for i in range(ring)]
    up = [(i, (i + 1) % ring) for i in range(ring)]

    cos_table, sin_table = rope_tables(jnp.arange(tokens, dtype=jnp.int32))
    cos_full = jnp.repeat(cos_table, 2, axis=1)
    sin_full = jnp.stack([-sin_table, sin_table], axis=-1).reshape(tokens, HEAD_DIM)

    query_all = jnp.zeros((tokens, head_width), jnp.float32)
    pair_all = jnp.zeros((tokens, 2 * HEAD_DIM), jnp.float32)
    held = hidden
    for step in range(ring):
        later = lax.ppermute(held, "tp", down) if step < ring - 1 else None
        query = jnp.dot(held, w_query, preferred_element_type=jnp.float32)
        key = jnp.dot(held, w_key, preferred_element_type=jnp.float32)
        value = jnp.dot(held, w_value, preferred_element_type=jnp.float32)
        segments = []
        for segment in range(seq_size):
            pair = slice(segment // share * HEAD_DIM, (segment // share + 1) * HEAD_DIM)
            segments.append(
                jnp.concatenate(
                    [
                        query[:, segment * head_width : (segment + 1) * head_width],
                        key[:, pair],
                        value[:, pair],
                    ],
                    axis=1,
                )
            )
        mine = scatter_heads(segments, seq_size, seq_rank)
        start = (place + step) % ring * rows
        query_all = lax.dynamic_update_slice_in_dim(query_all, mine[:, :head_width], start, 0)
        pair_all = lax.dynamic_update_slice_in_dim(pair_all, mine[:, head_width:], start, 0)
        held = later

    attended = attend(
        query_all,
        pair_all,
        cos_full,
        sin_full,
        (vert_blocks, vert_count, slash_offsets, slash_count),
    )

    gathered = []
    for step in range(ring):
        start = (place + 2 * ring - 1 - step) % ring * rows
        piece = lax.dynamic_slice_in_dim(attended, start, rows, 0)
        gathered.append(gather_heads(piece, seq_size, seq_rank))
    got = None
    for step in range(ring):
        term = jnp.dot(gathered[step], w_out, preferred_element_type=jnp.float32)
        if step > 0:
            term = term + got.astype(jnp.float32)
        term = term.astype(jnp.bfloat16)
        if step < ring - 1:
            got = lax.ppermute(term, "tp", up)
    return term


def solution(mesh):
    in_specs = (
        P(("groups", "tp"), "seq"),
        P("seq", "tp"),
        P("seq", "tp"),
        P("seq", "tp"),
        P("tp", "seq"),
        P(("groups", "tp"), None),
        P(("groups", "tp")),
        P(("groups", "tp"), None),
        P(("groups", "tp")),
    )
    out_specs = P(("groups", "tp"), "seq")
    return jax.shard_map(
        on_device, mesh=mesh, in_specs=in_specs, out_specs=out_specs, check_vma=False
    )
```

```python
import functools
import math

import jax
import jax.numpy as jnp
from jax import lax
from jax.experimental import pallas as pl
from jax.experimental.pallas import tpu as pltpu
from jax.sharding import PartitionSpec as P

HEAD_DIM = 128
BLOCK = 128
VERT = 3
SLASH = 3
PARTS = 2


NEG_FILL = -1e30


def rope_tables(positions):
    pair_index = jnp.arange(HEAD_DIM // 2, dtype=jnp.float32)
    base_freq = jnp.exp(-(2.0 * pair_index / HEAD_DIM) * jnp.log(500000.0))
    wavelength = 2.0 * jnp.pi / base_freq
    smooth = (8192.0 / wavelength - 1.0) / 3.0
    blended = (1.0 - smooth) * base_freq / 8.0 + smooth * base_freq
    scaled = jnp.where(
        wavelength < 2048.0, base_freq, jnp.where(wavelength > 8192.0, base_freq / 8.0, blended)
    )
    angles = positions.astype(jnp.float32)[:, None] * scaled[None, :]
    return (jnp.cos(angles), jnp.sin(angles))


def attend_kernel(
    heads_here,
    query_ref,
    pair_ref,
    cos_ref,
    sin_ref,
    vert_ref,
    vert_live_ref,
    slash_ref,
    slash_live_ref,
    out_ref,
    key_ref,
    value_ref,
):
    tokens = query_ref.shape[0]
    blocks = tokens // BLOCK
    score_scale = 1.0 / math.sqrt(HEAD_DIM)
    even = lax.broadcasted_iota(jnp.int32, (tokens, HEAD_DIM), 1) % 2 == 0

    def rotate(raw):
        swapped = jnp.where(
            even, pltpu.roll(raw, HEAD_DIM - 1, 1), pltpu.roll(raw, 1, 1)
        )
        return (raw * cos_ref[...] + swapped * sin_ref[...]).astype(jnp.bfloat16)

    @pl.when(pl.program_id(0) == 0)
    def _():
        key_ref[...] = rotate(pair_ref[:, :HEAD_DIM])
        value_ref[...] = pair_ref[:, HEAD_DIM:].astype(jnp.bfloat16)

    head = lax.axis_index("seq") * heads_here + pl.program_id(0)
    vert_live = vert_live_ref[head]
    slash_live = slash_live_ref[head]

    def listed(list_ref, live, slots, block):
        found = jnp.int32(0)
        for slot in range(slots):
            hit = (list_ref[head, slot] == block) & (live > slot)
            found = found | hit.astype(jnp.int32)
        return found

    vert_member = [listed(vert_ref, vert_live, VERT, block) for block in range(blocks)]
    slash_member = [listed(slash_ref, slash_live, SLASH, block) for block in range(blocks)]
    query = rotate(query_ref[...])
    causal = lax.broadcasted_iota(jnp.int32, (BLOCK, BLOCK), 1) <= lax.broadcasted_iota(
        jnp.int32, (BLOCK, BLOCK), 0
    )
    for row in range(blocks):
        width = (row + 1) * BLOCK
        scores = (
            lax.dot_general(
                query[row * BLOCK : width],
                key_ref[:width],
                (((1,), (1,)), ((), ())),
                preferred_element_type=jnp.float32,
            )
            * score_scale
        )
        masked = []
        for block in range(row + 1):
            visible = vert_member[block] | slash_member[row - block]
            bias = jnp.where(visible > 0, jnp.float32(0.0), jnp.float32(NEG_FILL))
            piece = scores[:, block * BLOCK : (block + 1) * BLOCK] + bias
            if block == row:
                piece = jnp.where(causal, piece, NEG_FILL)
            masked.append(piece)
        masked = masked[0] if row == 0 else jnp.concatenate(masked, axis=1)
        row_max = jnp.max(masked, axis=1, keepdims=True)
        weights = jnp.exp(masked - row_max)
        row_sum = jnp.sum(weights, axis=1, keepdims=True)
        weights_low = (weights / row_sum).astype(jnp.bfloat16)
        out_ref[row * BLOCK : width, :] = jnp.dot(
            weights_low, value_ref[:width], preferred_element_type=jnp.float32
        ).astype(jnp.bfloat16)


def attend(query_all, pair_all, cos_full, sin_full, lists):
    tokens, width = query_all.shape
    heads_here = width // HEAD_DIM
    whole = lambda head: (0, 0)
    one_head = lambda head: (0, head)
    return pl.pallas_call(
        functools.partial(attend_kernel, heads_here),
        grid=(heads_here,),
        out_shape=jax.ShapeDtypeStruct((tokens, width), jnp.bfloat16),
        in_specs=[
            pl.BlockSpec((tokens, HEAD_DIM), one_head),
            pl.BlockSpec((tokens, 2 * HEAD_DIM), whole),
            pl.BlockSpec((tokens, HEAD_DIM), whole),
            pl.BlockSpec((tokens, HEAD_DIM), whole),
        ]
        + [pl.BlockSpec(memory_space=pltpu.SMEM)] * 4,
        out_specs=pl.BlockSpec((tokens, HEAD_DIM), one_head),
        scratch_shapes=[
            pltpu.VMEM((tokens, HEAD_DIM), jnp.bfloat16),
            pltpu.VMEM((tokens, HEAD_DIM), jnp.bfloat16),
        ],
        compiler_params=pltpu.CompilerParams(vmem_limit_bytes=40 * 1024 * 1024),
    )(query_all, pair_all, cos_full, sin_full, *lists)


def swap_with(value, bit, size):
    return lax.ppermute(value, "seq", [(rank, rank ^ bit) for rank in range(size)])


def halve(segments, bit, size, rank):
    low = (rank // bit) % 2 == 0
    count = len(segments) // 2
    kept = [jnp.where(low, segments[2 * i], segments[2 * i + 1]) for i in range(count)]
    sent = [jnp.where(low, segments[2 * i + 1], segments[2 * i]) for i in range(count)]
    return kept, swap_with(jnp.concatenate(sent, axis=1), bit, size)


def join_halves(kept, got):
    width = kept[0].shape[1]
    return [mine + got[:, i * width : (i + 1) * width] for i, mine in enumerate(kept)]


def widen(segments, got, bit, rank):
    low = (rank // bit) % 2 == 0
    width = segments[0].shape[1]
    wider = []
    for i, mine in enumerate(segments):
        other = got[:, i * width : (i + 1) * width]
        wider += [jnp.where(low, mine, other), jnp.where(low, other, mine)]
    return wider


def gather_rest(piece, got, size, rank):
    bit = size // 2
    segments = widen([piece], got, bit, rank)
    while bit > 1:
        bit //= 2
        got = swap_with(jnp.concatenate(segments, axis=1), bit, size)
        segments = widen(segments, got, bit, rank)
    return jnp.concatenate(segments, axis=1)


def on_device(
    hidden, w_query, w_key, w_value, w_out, vert_blocks, vert_count, slash_offsets, slash_count
):
    seq_size = lax.axis_size("seq")
    seq_rank = lax.axis_index("seq")
    ring = lax.axis_size("tp")
    place = lax.axis_index("tp")
    rows = hidden.shape[0]
    tokens = rows * ring
    head_width = w_query.shape[1] // seq_size
    pairs = w_key.shape[1] // HEAD_DIM
    share = seq_size // pairs
    down = [(i, (i - 1) % ring) for i in range(ring)]
    up = [(i, (i + 1) % ring) for i in range(ring)]

    cos_table, sin_table = rope_tables(jnp.arange(tokens, dtype=jnp.int32))
    cos_full = jnp.repeat(cos_table, 2, axis=1)
    sin_full = jnp.stack([-sin_table, sin_table], axis=-1).reshape(tokens, HEAD_DIM)

    query_all = jnp.zeros((tokens, head_width), jnp.float32)
    pair_all = jnp.zeros((tokens, 2 * HEAD_DIM), jnp.float32)
    stages = [1 << i for i in range(seq_size.bit_length() - 1)]
    flying = []
    done = [None] * ring
    held = hidden
    for step in range(ring + len(stages)):
        query = None
        if step < ring:
            later = lax.ppermute(held, "tp", down) if step < ring - 1 else None
            query = jnp.dot(held, w_query, preferred_element_type=jnp.float32)
            key = jnp.dot(held, w_key, preferred_element_type=jnp.float32)
            value = jnp.dot(held, w_value, preferred_element_type=jnp.float32)
            if flying:
                landed, query = lax.optimization_barrier(([entry[3] for entry in flying], query))
                flying = [entry[:3] + (got,) for entry, got in zip(flying, landed)]
        moved = []
        for block, stage, kept, got in flying:
            segments = join_halves(kept, got)
            if stage + 1 < len(stages):
                moved.append((block, stage + 1, segments))
            else:
                done[block] = segments[0]
        if query is not None:
            segments = []
            for segment in range(seq_size):
                pair = slice(segment // share * HEAD_DIM, (segment // share + 1) * HEAD_DIM)
                segments.append(
                    jnp.concatenate(
                        [
                            query[:, segment * head_width : (segment + 1) * head_width],
                            key[:, pair],
                            value[:, pair],
                        ],
                        axis=1,
                    )
                )
            moved.append((step, 0, segments))
            held = later
        flying = []
        for block, stage, segments in moved:
            kept, got = halve(segments, stages[stage], seq_size, seq_rank)
            flying.append((block, stage, kept, got))
    for step, mine in enumerate(done):
        start = (place + step) % ring * rows
        query_all = lax.dynamic_update_slice_in_dim(query_all, mine[:, :head_width], start, 0)
        pair_all = lax.dynamic_update_slice_in_dim(pair_all, mine[:, head_width:], start, 0)

    attended = attend(
        query_all,
        pair_all,
        cos_full,
        sin_full,
        (vert_blocks, vert_count, slash_offsets, slash_count),
    )

    pieces, halfway = [], []
    for step in range(ring):
        start = (place + 2 * ring - 1 - step) % ring * rows
        pieces.append(lax.dynamic_slice_in_dim(attended, start, rows, 0))
        halfway.append(swap_with(pieces[step], seq_size // 2, seq_size))
    columns = w_out.shape[1] // PARTS
    got = [None] * PARTS
    gathered = gather_rest(pieces[0], halfway[0], seq_size, seq_rank)
    for step in range(ring):
        terms = []
        for part in range(PARTS):
            term = jnp.dot(
                gathered,
                w_out[:, part * columns : (part + 1) * columns],
                preferred_element_type=jnp.float32,
            )
            if part == 0 and step + 1 < ring:
                landed, term = lax.optimization_barrier((halfway[step + 1], term))
                following = gather_rest(pieces[step + 1], landed, seq_size, seq_rank)
            if step > 0:
                term, arrived = lax.optimization_barrier((term, got[part]))
                term = term + arrived.astype(jnp.float32)
            term = term.astype(jnp.bfloat16)
            if part + 1 < PARTS:
                gathered, term = lax.optimization_barrier((gathered, term))
            elif step + 1 < ring:
                gathered, term = lax.optimization_barrier((following, term))
            terms.append(term)
            if step < ring - 1:
                got[part] = lax.ppermute(term, "tp", up)
    return jnp.concatenate(terms, axis=1)


def solution(mesh):
    in_specs = (
        P(("groups", "tp"), "seq"),
        P("seq", "tp"),
        P("seq", "tp"),
        P("seq", "tp"),
        P("tp", "seq"),
        P(("groups", "tp"), None),
        P(("groups", "tp")),
        P(("groups", "tp"), None),
        P(("groups", "tp")),
    )
    out_specs = P(("groups", "tp"), "seq")
    return jax.shard_map(
        on_device, mesh=mesh, in_specs=in_specs, out_specs=out_specs, check_vma=False
    )
```

```python
import functools
import math

import jax
import jax.numpy as jnp
from jax import lax
from jax.experimental import pallas as pl
from jax.experimental.pallas import tpu as pltpu
from jax.sharding import PartitionSpec as P

HEAD_DIM = 128
BLOCK = 128
VERT = 3
SLASH = 3
PARTS = 2


NEG_FILL = -1e30


def rope_tables(positions):
    pair_index = jnp.arange(HEAD_DIM // 2, dtype=jnp.float32)
    base_freq = jnp.exp(-(2.0 * pair_index / HEAD_DIM) * jnp.log(500000.0))
    wavelength = 2.0 * jnp.pi / base_freq
    smooth = (8192.0 / wavelength - 1.0) / 3.0
    blended = (1.0 - smooth) * base_freq / 8.0 + smooth * base_freq
    scaled = jnp.where(
        wavelength < 2048.0, base_freq, jnp.where(wavelength > 8192.0, base_freq / 8.0, blended)
    )
    angles = positions.astype(jnp.float32)[:, None] * scaled[None, :]
    return (jnp.cos(angles), jnp.sin(angles))


def attend_kernel(
    heads_here,
    query_ref,
    pair_ref,
    cos_ref,
    sin_ref,
    vert_ref,
    vert_live_ref,
    slash_ref,
    slash_live_ref,
    out_ref,
    key_ref,
    value_ref,
):
    tokens = query_ref.shape[0]
    blocks = tokens // BLOCK
    score_scale = 1.0 / math.sqrt(HEAD_DIM)
    even = lax.broadcasted_iota(jnp.int32, (tokens, HEAD_DIM), 1) % 2 == 0

    def rotate(raw):
        swapped = jnp.where(
            even, pltpu.roll(raw, HEAD_DIM - 1, 1), pltpu.roll(raw, 1, 1)
        )
        return (raw * cos_ref[...] + swapped * sin_ref[...]).astype(jnp.bfloat16)

    @pl.when(pl.program_id(0) == 0)
    def _():
        key_ref[...] = rotate(pair_ref[:, :HEAD_DIM])
        value_ref[...] = pair_ref[:, HEAD_DIM:].astype(jnp.bfloat16)

    head = lax.axis_index("seq") * heads_here + pl.program_id(0)
    vert_live = vert_live_ref[head]
    slash_live = slash_live_ref[head]

    def listed(list_ref, live, slots, block):
        found = jnp.int32(0)
        for slot in range(slots):
            hit = (list_ref[head, slot] == block) & (live > slot)
            found = found | hit.astype(jnp.int32)
        return found

    vert_member = [listed(vert_ref, vert_live, VERT, block) for block in range(blocks)]
    slash_member = [listed(slash_ref, slash_live, SLASH, block) for block in range(blocks)]
    query = rotate(query_ref[...])
    causal = lax.broadcasted_iota(jnp.int32, (BLOCK, BLOCK), 1) <= lax.broadcasted_iota(
        jnp.int32, (BLOCK, BLOCK), 0
    )
    for row in range(blocks):
        width = (row + 1) * BLOCK
        scores = (
            lax.dot_general(
                query[row * BLOCK : width],
                key_ref[:width],
                (((1,), (1,)), ((), ())),
                preferred_element_type=jnp.float32,
            )
            * score_scale
        )
        masked = []
        for block in range(row + 1):
            visible = vert_member[block] | slash_member[row - block]
            bias = jnp.where(visible > 0, jnp.float32(0.0), jnp.float32(NEG_FILL))
            piece = scores[:, block * BLOCK : (block + 1) * BLOCK] + bias
            if block == row:
                piece = jnp.where(causal, piece, NEG_FILL)
            masked.append(piece)
        masked = masked[0] if row == 0 else jnp.concatenate(masked, axis=1)
        row_max = jnp.max(masked, axis=1, keepdims=True)
        weights = jnp.exp(masked - row_max)
        row_sum = jnp.sum(weights, axis=1, keepdims=True)
        weights_low = (weights / row_sum).astype(jnp.bfloat16)
        out_ref[row * BLOCK : width, :] = jnp.dot(
            weights_low, value_ref[:width], preferred_element_type=jnp.float32
        ).astype(jnp.bfloat16)


def attend(query_all, pair_all, cos_full, sin_full, lists):
    tokens, width = query_all.shape
    heads_here = width // HEAD_DIM
    whole = lambda head: (0, 0)
    one_head = lambda head: (0, head)
    return pl.pallas_call(
        functools.partial(attend_kernel, heads_here),
        grid=(heads_here,),
        out_shape=jax.ShapeDtypeStruct((tokens, width), jnp.bfloat16),
        in_specs=[
            pl.BlockSpec((tokens, HEAD_DIM), one_head),
            pl.BlockSpec((tokens, 2 * HEAD_DIM), whole),
            pl.BlockSpec((tokens, HEAD_DIM), whole),
            pl.BlockSpec((tokens, HEAD_DIM), whole),
        ]
        + [pl.BlockSpec(memory_space=pltpu.SMEM)] * 4,
        out_specs=pl.BlockSpec((tokens, HEAD_DIM), one_head),
        scratch_shapes=[
            pltpu.VMEM((tokens, HEAD_DIM), jnp.bfloat16),
            pltpu.VMEM((tokens, HEAD_DIM), jnp.bfloat16),
        ],
        compiler_params=pltpu.CompilerParams(vmem_limit_bytes=40 * 1024 * 1024),
    )(query_all, pair_all, cos_full, sin_full, *lists)


def swap_with(value, bit, size):
    return lax.ppermute(value, "seq", [(rank, rank ^ bit) for rank in range(size)])


def halve(segments, bit, size, rank):
    low = (rank // bit) % 2 == 0
    count = len(segments) // 2
    kept = [jnp.where(low, segments[2 * i], segments[2 * i + 1]) for i in range(count)]
    sent = [jnp.where(low, segments[2 * i + 1], segments[2 * i]) for i in range(count)]
    return kept, swap_with(jnp.concatenate(sent, axis=1), bit, size)


def join_halves(kept, got):
    width = kept[0].shape[1]
    return [mine + got[:, i * width : (i + 1) * width] for i, mine in enumerate(kept)]


def widen(segments, got, bit, rank):
    low = (rank // bit) % 2 == 0
    width = segments[0].shape[1]
    wider = []
    for i, mine in enumerate(segments):
        other = got[:, i * width : (i + 1) * width]
        wider += [jnp.where(low, mine, other), jnp.where(low, other, mine)]
    return wider


def gather_rest(piece, got, size, rank):
    bit = size // 2
    segments = widen([piece], got, bit, rank)
    while bit > 1:
        bit //= 2
        got = swap_with(jnp.concatenate(segments, axis=1), bit, size)
        segments = widen(segments, got, bit, rank)
    return jnp.concatenate(segments, axis=1)


def on_device(
    hidden, w_query, w_key, w_value, w_out, vert_blocks, vert_count, slash_offsets, slash_count
):
    seq_size = lax.axis_size("seq")
    seq_rank = lax.axis_index("seq")
    ring = lax.axis_size("tp")
    place = lax.axis_index("tp")
    rows = hidden.shape[0]
    tokens = rows * ring
    head_width = w_query.shape[1] // seq_size
    pairs = w_key.shape[1] // HEAD_DIM
    share = seq_size // pairs
    down = [(i, (i - 1) % ring) for i in range(ring)]
    up = [(i, (i + 1) % ring) for i in range(ring)]

    cos_table, sin_table = rope_tables(jnp.arange(tokens, dtype=jnp.int32))
    cos_full = jnp.repeat(cos_table, 2, axis=1)
    sin_full = jnp.stack([-sin_table, sin_table], axis=-1).reshape(tokens, HEAD_DIM)

    query_all = jnp.zeros((tokens, head_width), jnp.float32)
    pair_all = jnp.zeros((tokens, 2 * HEAD_DIM), jnp.float32)
    stages = [1 << i for i in range(seq_size.bit_length() - 1)]
    flying = []
    done = [None] * ring
    held = hidden
    for step in range(ring + len(stages)):
        query = None
        if step < ring:
            later = lax.ppermute(held, "tp", down) if step < ring - 1 else None
            query = jnp.dot(held, w_query, preferred_element_type=jnp.float32)
            key = jnp.dot(held, w_key, preferred_element_type=jnp.float32)
            value = jnp.dot(held, w_value, preferred_element_type=jnp.float32)
            if flying:
                landed, query = lax.optimization_barrier(([entry[3] for entry in flying], query))
                flying = [entry[:3] + (got,) for entry, got in zip(flying, landed)]
        moved = []
        for block, stage, kept, got in flying:
            segments = join_halves(kept, got)
            if stage + 1 < len(stages):
                moved.append((block, stage + 1, segments))
            else:
                done[block] = segments[0]
        if query is not None:
            segments = []
            for segment in range(seq_size):
                pair = slice(segment // share * HEAD_DIM, (segment // share + 1) * HEAD_DIM)
                segments.append(
                    jnp.concatenate(
                        [
                            query[:, segment * head_width : (segment + 1) * head_width],
                            key[:, pair],
                            value[:, pair],
                        ],
                        axis=1,
                    )
                )
            moved.append((step, 0, segments))
            held = later
        flying = []
        for block, stage, segments in moved:
            kept, got = halve(segments, stages[stage], seq_size, seq_rank)
            flying.append((block, stage, kept, got))
    for step, mine in enumerate(done):
        start = (place + step) % ring * rows
        query_all = lax.dynamic_update_slice_in_dim(query_all, mine[:, :head_width], start, 0)
        pair_all = lax.dynamic_update_slice_in_dim(pair_all, mine[:, head_width:], start, 0)

    attended = attend(
        query_all,
        pair_all,
        cos_full,
        sin_full,
        (vert_blocks, vert_count, slash_offsets, slash_count),
    )

    pieces, halfway = [], []
    for step in range(ring):
        start = (place + 2 * ring - 1 - step) % ring * rows
        pieces.append(lax.dynamic_slice_in_dim(attended, start, rows, 0))
        halfway.append(swap_with(pieces[step], seq_size // 2, seq_size))
    columns = w_out.shape[1] // PARTS
    got = [None] * PARTS
    gathered = gather_rest(pieces[0], halfway[0], seq_size, seq_rank)
    for step in range(ring):
        terms = []
        for part in range(PARTS):
            if step > 0:
                gathered, got[part] = lax.optimization_barrier((gathered, got[part]))
            term = jnp.dot(
                gathered,
                w_out[:, part * columns : (part + 1) * columns],
                preferred_element_type=jnp.float32,
            )
            if part == 0 and step + 1 < ring:
                landed = halfway[step + 1]
                if step > 0:
                    landed, term = lax.optimization_barrier((landed, term))
                following = gather_rest(pieces[step + 1], landed, seq_size, seq_rank)
            if step > 0:
                term, arrived = lax.optimization_barrier((term, got[part]))
                term = term + arrived.astype(jnp.float32)
            term = term.astype(jnp.bfloat16)
            if part + 1 < PARTS:
                gathered, term = lax.optimization_barrier((gathered, term))
            elif step + 1 < ring:
                gathered, term = lax.optimization_barrier((following, term))
            terms.append(term)
            if step < ring - 1:
                got[part] = lax.ppermute(term, "tp", up)
    return jnp.concatenate(terms, axis=1)


def solution(mesh):
    in_specs = (
        P(("groups", "tp"), "seq"),
        P("seq", "tp"),
        P("seq", "tp"),
        P("seq", "tp"),
        P("tp", "seq"),
        P(("groups", "tp"), None),
        P(("groups", "tp")),
        P(("groups", "tp"), None),
        P(("groups", "tp")),
    )
    out_specs = P(("groups", "tp"), "seq")
    return jax.shard_map(
        on_device, mesh=mesh, in_specs=in_specs, out_specs=out_specs, check_vma=False
    )
```
